32 devices in a mesh: row: 16 (over z, y, core), col: 2 (over x).
Axes of the slice: x: 2, y: 2, z: 4, core: 2. Of those that a mesh axis runs over, the one named last changes fastest.
Arguments:
- slab: bfloat16 [16384, 4096], P('row', 'col'), may hold values from -6 to 6
- panel_left: bfloat16 [16384, 512], P('row', 'col'), may hold values from -3 to 3
- panel_top: bfloat16 [512, 4096], P('row', 'col'), may hold values from -3 to 3
- row_bases: bfloat16 [16384, 256], P('row'), may hold values from -0.25 to 0.25
- col_bases: bfloat16 [4096, 256], P('col'), may hold values from -0.25 to 0.25
- row_ranks: int32 [32], P('row'), may hold values from 32 to 256, as said below
- col_ranks: int32 [8], P('col'), may hold values from 32 to 256, as said below
- pivot_inverse: bfloat16 [512, 512], replicated, may hold values from -0.0625 to 0.0625
- pivot_rhs: bfloat16 [512, 1024], P('row', 'col'), may hold values from -6 to 6
- rhs: bfloat16 [16384, 1024], P('row', 'col'), may hold values from -6 to 6
Outputs:
- slab_new: bfloat16 [16384, 4096], P('row', 'col')
- rhs_new: bfloat16 [16384, 1024], P('row', 'col')
The draws below stay inside these ranges and needn't reach their ends.
Inputs may be any that keep to these rules, and one draw needn't show every extreme that they name: `row_ranks`: each entry is the rank of one tile; the value 256 occurs in every draw. `col_ranks`: each entry is the rank of one tile; the value 256 occurs in every draw.
All inputs are finite; a program needn't handle non-finite values.
Results may differ from the reference program's by a relative error of at most 0.0062.
Values may be sent and summed in bfloat16 or wider, within the bound.
A program may use at most 128 MiB of HBM per device.

```python
import jax
import jax.numpy as jnp
from jax import lax

B = 512
RMAX = 256
LOW_RANK = 32
ROW_TILES = 32
COL_TILES = 8
ROWS = 16384
COLS = 4096
GAINS = 1024


def spread_ranks(key, count):
    first_key, second_key = jax.random.split(jax.random.fold_in(key, 17))
    values = jax.random.randint(first_key, (count,), LOW_RANK, RMAX + 1).astype(jnp.int32)
    where = jax.random.randint(second_key, (), 0, count).astype(jnp.int32)
    values = values.at[where].set(RMAX)
    return values


def draw_row_ranks(key, part):
    return spread_ranks(jax.random.fold_in(key, 101), ROW_TILES)


def draw_col_ranks(key, part):
    return spread_ranks(jax.random.fold_in(key, 202), COL_TILES)


def block_scale(rng, shape, pieces, least, top_value):
    level = 1.0
    for position, parts in pieces:
        draws = jax.random.uniform(jax.random.fold_in(jax.random.fold_in(rng, 6), position), (parts,), jnp.float32, least / len(pieces), top_value / len(pieces))
        level = level * jnp.repeat(jnp.exp(draws), shape[position] // parts).reshape((-1,) + (1,) * (len(shape) - 1 - position))
    return level


def gaussian(key, shape, scale, bound, shards=(), kind=jnp.bfloat16):
    level = block_scale(key, shape, shards, -0.22, 0.18) if shards else 1.0
    array = jax.random.normal(key, shape, jnp.float32) * scale * level
    return jnp.minimum(jnp.maximum(array, -bound), bound).astype(kind)


def setup_inputs(seed: int = 0) -> dict:
    key_list = jax.random.split(jax.random.key(seed), 11)
    return {
        "slab": gaussian(key_list[0], (ROWS, COLS), 1.0, 6.0, ((0, 16), (1, 2))),
        "panel_left": gaussian(key_list[1], (ROWS, B), 0.4, 3.0, ((0, 16), (1, 2))),
        "panel_top": gaussian(key_list[2], (B, COLS), 0.4, 3.0, ((0, 16), (1, 2))),
        "row_bases": gaussian(key_list[3], (ROWS, RMAX), B ** -0.5, 0.25, ((0, 16),)),
        "col_bases": gaussian(key_list[4], (COLS, RMAX), B ** -0.5, 0.25, ((0, 2),)),
        "row_ranks": draw_row_ranks(jax.random.fold_in(key_list[10], 71), 0),
        "col_ranks": draw_col_ranks(jax.random.fold_in(key_list[10], 71), 0),
        "pivot_inverse": gaussian(key_list[7], (B, B), (16 * B) ** -0.5, 0.0625),
        "pivot_rhs": gaussian(key_list[8], (B, GAINS), 1.0, 6.0, ((0, 16), (1, 2))),
        "rhs": gaussian(key_list[9], (ROWS, GAINS), 1.0, 6.0, ((0, 16), (1, 2))),
    }


def reference(slab, panel_left, panel_top, row_bases, col_bases, row_ranks, col_ranks, pivot_inverse, pivot_rhs, rhs):
    levels = jnp.arange(RMAX, dtype=jnp.int32)
    keep_row = (levels[None, :] < row_ranks[:, None]).astype(jnp.float32)
    keep_column = (levels[None, :] < col_ranks[:, None]).astype(jnp.float32)
    left_bases = row_bases.reshape(ROW_TILES, B, RMAX).astype(jnp.float32)
    right_bases = col_bases.reshape(COL_TILES, B, RMAX).astype(jnp.float32)
    left_tiles = panel_left.reshape(ROW_TILES, B, B).astype(jnp.float32)
    row_core = (jnp.einsum("tbr,tbc->trc", left_bases, left_tiles) * keep_row[:, :, None]).astype(jnp.bfloat16)
    upper_rows = panel_top.reshape(B, COL_TILES, B).astype(jnp.float32)
    column_core = (jnp.einsum("pjc,jcr->pjr", upper_rows, right_bases) * keep_column[None]).astype(jnp.bfloat16)
    column_wide = column_core.astype(jnp.float32)
    slab_tiles = slab.reshape(ROW_TILES, B, COLS)

    def one_row(packed):
        core_rows, basis, block = packed
        core_block = jnp.einsum("rp,pjs->jrs", core_rows.astype(jnp.float32), column_wide).astype(jnp.bfloat16)
        spread = jnp.einsum("br,jrs->jbs", basis, core_block.astype(jnp.float32)).astype(jnp.bfloat16)
        change = jnp.einsum("jbs,jcs->bjc", spread.astype(jnp.float32), right_bases).reshape(B, COLS)
        return (block.astype(jnp.float32) - change).astype(jnp.bfloat16)

    slab_new = lax.map(one_row, (row_core, left_bases, slab_tiles)).reshape(ROWS, COLS)
    pivot_solution = jnp.dot(pivot_inverse, pivot_rhs, preferred_element_type=jnp.float32).astype(jnp.bfloat16)
    reduced = jnp.einsum("irp,pg->irg", row_core.astype(jnp.float32), pivot_solution.astype(jnp.float32)).astype(jnp.bfloat16)
    lowered = jnp.einsum("ibr,irg->ibg", left_bases, reduced.astype(jnp.float32)).reshape(ROWS, GAINS)
    rhs_new = (rhs.astype(jnp.float32) - lowered).astype(jnp.bfloat16)
    return slab_new, rhs_new
```

```python
import functools

import jax
import jax.numpy as jnp
from jax import lax
from jax.experimental import pallas as pl
from jax.experimental.pallas import tpu as pltpu
from jax.sharding import PartitionSpec as P

MESH = pl.DeviceIdType.MESH


def grid_of(count):
    cores = 2 if count % 2 == 0 else 1
    chips = count // cores
    inner = max(d for d in range(1, chips + 1) if chips % d == 0 and d * d <= chips)
    return chips // inner, inner, cores


def gather_kernel(
    n_row,
    n_col,
    col_ranks,
    row_ranks,
    top,
    right,
    left,
    bases,
    inverse,
    pivot,
    core_out,
    reduced_out,
    blocks,
    cores_k,
    block_send,
    block_recv,
    k_send,
    k_recv,
):
    outer, inner, cores = grid_of(n_row)
    order = inverse.shape[0]
    rank = bases.shape[1]
    n_tiles = row_ranks.shape[0]
    m_tiles = col_ranks.shape[0]
    width = left.shape[1]
    m_width = m_tiles * rank

    row = lax.axis_index("row")
    col = lax.axis_index("col")
    c = lax.rem(row, cores)
    b = lax.rem(row // cores, inner)
    a = row // (cores * inner)

    def index(a_, b_, c_):
        return (a_ * inner + b_) * cores + c_

    a_peers = [lax.rem(a + k, outer) for k in range(1, outer)]
    b_peers = [lax.rem(b + k, inner) for k in range(1, inner)]
    c_peers = [lax.rem(c + k, cores) for k in range(1, cores)]
    col_peers = [lax.rem(col + k, n_col) for k in range(1, n_col)]

    barrier = pltpu.get_barrier_semaphore()
    partners = [(index(p, b, c), col) for p in a_peers]
    partners += [(index(a, p, c), col) for p in b_peers]
    partners += [(index(a, b, p), col) for p in c_peers]
    partners += [(row, p) for p in col_peers]
    for partner in partners:
        pl.semaphore_signal(barrier, inc=1, device_id=partner, device_id_type=MESH)

    levels = lax.broadcasted_iota(jnp.int32, (1, rank), 1)
    for j in range(m_tiles):
        part = jnp.dot(
            top[:, j * order : (j + 1) * order],
            right[j * order : (j + 1) * order, :],
            preferred_element_type=jnp.float32,
        )
        part = jnp.where(levels < col_ranks[j], part, 0.0)
        blocks[row, :, j * rank : (j + 1) * rank] = part.astype(jnp.bfloat16)
    blocks[row, :, m_width:] = pivot[...]

    pl.semaphore_wait(barrier, len(partners))
    started = []

    def send(which, target):
        copy = pltpu.make_async_remote_copy(
            src_ref=blocks.at[which],
            dst_ref=blocks.at[which],
            send_sem=block_send.at[len(started)],
            recv_sem=block_recv.at[which],
            device_id=(target, col),
            device_id_type=MESH,
        )
        copy.start()
        started.append(copy)

    def arrived(which):
        pltpu.make_async_copy(blocks.at[which], blocks.at[which], block_recv.at[which]).wait()

    for p in reversed(a_peers):
        send(row, index(p, b, c))
    for p in b_peers:
        send(row, index(a, p, c))
    for p in c_peers:
        send(row, index(a, b, p))

    rows = lax.broadcasted_iota(jnp.int32, (rank, 1), 0)
    for i in range(n_tiles):
        part = lax.dot_general(
            bases[i * order : (i + 1) * order, :],
            left[i * order : (i + 1) * order, :],
            (((0,), (0,)), ((), ())),
            preferred_element_type=jnp.float32,
        )
        part = jnp.where(rows < row_ranks[i], part, 0.0)
        cores_k[col, i] = part.astype(jnp.bfloat16)
    k_copies = []
    for number, p in enumerate(col_peers):
        copy = pltpu.make_async_remote_copy(
            src_ref=cores_k.at[col],
            dst_ref=cores_k.at[col],
            send_sem=k_send.at[number],
            recv_sem=k_recv.at[col],
            device_id=(row, p),
            device_id_type=MESH,
        )
        copy.start()
        k_copies.append(copy)

    def from_inner(a_):
        for p in b_peers:
            s = index(a_, p, c)
            arrived(s)
            for q in c_peers:
                send(s, index(a, b, q))

    previous = a
    for p in a_peers:
        s = index(p, b, c)
        arrived(s)
        for q in b_peers:
            send(s, index(a, q, c))
        for q in c_peers:
            send(s, index(a, b, q))
        from_inner(previous)
        previous = p

    for p in col_peers:
        pltpu.make_async_copy(cores_k.at[p], cores_k.at[p], k_recv.at[p]).wait()
    solvers = []
    for i in range(n_tiles):
        total = jnp.zeros((rank, order), jnp.float32)
        for k in range(n_col):
            total += jnp.dot(
                cores_k[k, i],
                inverse[k * width : (k + 1) * width, :],
                preferred_element_type=jnp.float32,
            )
        solvers.append(total.astype(jnp.bfloat16))

    from_inner(previous)
    for q in c_peers:
        for p in [a] + a_peers:
            for r in [b] + b_peers:
                arrived(index(p, r, q))

    depth = blocks.shape[1]
    share = n_row // n_col
    wide = blocks.shape[2]
    for i in range(n_tiles):
        total = jnp.zeros((rank, m_width), jnp.float32)
        for k in range(n_col):
            piece = blocks[k * share : (k + 1) * share, :, :m_width]
            total += jnp.dot(
                cores_k[k, i],
                piece.reshape(share * depth, m_width),
                preferred_element_type=jnp.float32,
            )
        core_out[i] = total.astype(jnp.bfloat16)
        gains = blocks[:, :, m_width:].reshape(order, wide - m_width)
        reduced_out[i] = jnp.dot(
            solvers[i], gains, preferred_element_type=jnp.float32
        ).astype(jnp.bfloat16)

    for copy in started + k_copies:
        copy.wait_send()


def update_kernel(bases, core, reduced, right, slab, rhs, slab_out, rhs_out):
    rank = bases.shape[1]
    m_tiles = core.shape[2] // rank
    order = right.shape[0] // m_tiles
    basis = bases[...]
    for j in range(m_tiles):
        spread = jnp.dot(
            basis, core[0, :, j * rank : (j + 1) * rank], preferred_element_type=jnp.float32
        ).astype(jnp.bfloat16)
        change = lax.dot_general(
            spread,
            right[j * order : (j + 1) * order, :],
            (((1,), (1,)), ((), ())),
            preferred_element_type=jnp.float32,
        )
        at = slice(j * order, (j + 1) * order)
        slab_out[:, at] = (slab[:, at].astype(jnp.float32) - change).astype(jnp.bfloat16)
    lowered = jnp.dot(basis, reduced[0], preferred_element_type=jnp.float32)
    rhs_out[...] = (rhs[...].astype(jnp.float32) - lowered).astype(jnp.bfloat16)


def per_device(
    n_row,
    n_col,
    slab,
    panel_left,
    panel_top,
    row_bases,
    col_bases,
    row_ranks,
    col_ranks,
    pivot_inverse,
    pivot_rhs,
    rhs,
):
    order = pivot_inverse.shape[0]
    rank = row_bases.shape[1]
    n_tiles = row_ranks.shape[0]
    m_tiles = col_ranks.shape[0]
    gains = rhs.shape[1]
    width = panel_left.shape[1]
    outer, inner, cores = grid_of(n_row)
    sends = (outer - 1) + outer * (inner - 1) + outer * inner * (cores - 1)
    vmem = pl.BlockSpec(memory_space=pltpu.VMEM)
    smem = pl.BlockSpec(memory_space=pltpu.SMEM)
    core, reduced = pl.pallas_call(
        functools.partial(gather_kernel, n_row, n_col),
        out_shape=(
            jax.ShapeDtypeStruct((n_tiles, rank, m_tiles * rank), jnp.bfloat16),
            jax.ShapeDtypeStruct((n_tiles, rank, gains), jnp.bfloat16),
        ),
        in_specs=[smem, smem] + [vmem] * 6,
        out_specs=(vmem, vmem),
        scratch_shapes=[
            pltpu.VMEM((n_row, pivot_rhs.shape[0], m_tiles * rank + gains), jnp.bfloat16),
            pltpu.VMEM((n_col, n_tiles, rank, width), jnp.bfloat16),
            pltpu.SemaphoreType.DMA((sends,)),
            pltpu.SemaphoreType.DMA((n_row,)),
            pltpu.SemaphoreType.DMA((max(n_col - 1, 1),)),
            pltpu.SemaphoreType.DMA((n_col,)),
        ],
        compiler_params=pltpu.CompilerParams(
            collective_id=0, has_side_effects=True, vmem_limit_bytes=24 * 2**20
        ),
        name="gather",
    )(col_ranks, row_ranks, panel_top, col_bases, panel_left, row_bases, pivot_inverse, pivot_rhs)

    step = order // 2
    per_tile = order // step
    rows, columns = slab.shape
    return pl.pallas_call(
        update_kernel,
        grid=(rows // step,),
        out_shape=(
            jax.ShapeDtypeStruct(slab.shape, slab.dtype),
            jax.ShapeDtypeStruct(rhs.shape, rhs.dtype),
        ),
        in_specs=[
            pl.BlockSpec((step, rank), lambda r: (r, 0)),
            pl.BlockSpec((1, rank, m_tiles * rank), lambda r: (r // per_tile, 0, 0)),
            pl.BlockSpec((1, rank, gains), lambda r: (r // per_tile, 0, 0)),
            pl.BlockSpec((columns, rank), lambda r: (0, 0)),
            pl.BlockSpec((step, columns), lambda r: (r, 0)),
            pl.BlockSpec((step, gains), lambda r: (r, 0)),
        ],
        out_specs=(
            pl.BlockSpec((step, columns), lambda r: (r, 0)),
            pl.BlockSpec((step, gains), lambda r: (r, 0)),
        ),
        compiler_params=pltpu.CompilerParams(vmem_limit_bytes=32 * 2**20),
        name="update",
    )(row_bases, core, reduced, col_bases, slab, rhs)


def solution(mesh):
    in_specs = (
        P("row", "col"),
        P("row", "col"),
        P("row", "col"),
        P("row", None),
        P("col", None),
        P("row"),
        P("col"),
        P(),
        P("row", "col"),
        P("row", "col"),
    )
    out_specs = (P("row", "col"), P("row", "col"))
    return jax.shard_map(
        functools.partial(per_device, mesh.shape["row"], mesh.shape["col"]),
        mesh=mesh,
        in_specs=in_specs,
        out_specs=out_specs,
        check_vma=False,
    )
```

```python
import functools

import jax
import jax.numpy as jnp
from jax import lax
from jax.experimental import pallas as pl
from jax.experimental.pallas import tpu as pltpu
from jax.sharding import PartitionSpec as P

MESH = pl.DeviceIdType.MESH


def grid_of(count):
    cores = 2 if count % 2 == 0 else 1
    chips = count // cores
    inner = max(d for d in range(1, chips + 1) if chips % d == 0 and d * d <= chips)
    return chips // inner, inner, cores


def gather_kernel(
    n_row,
    n_col,
    col_ranks_hbm,
    row_ranks_hbm,
    top_hbm,
    right_hbm,
    left_hbm,
    bases_hbm,
    inverse_hbm,
    pivot_hbm,
    core_out,
    reduced_out,
    col_ranks,
    row_ranks,
    top,
    right,
    left,
    bases,
    inverse,
    m_blocks,
    g_blocks,
    cores_k,
    load_sem,
    m_send,
    m_recv,
    g_send,
    g_recv,
    k_send,
    k_recv,
):
    outer, inner, cores = grid_of(n_row)
    order = inverse.shape[0]
    rank = bases.shape[1]
    n_tiles = row_ranks.shape[0]
    m_tiles = col_ranks.shape[0]
    width = left.shape[1]

    row = lax.axis_index("row")
    col = lax.axis_index("col")
    c = lax.rem(row, cores)
    b = lax.rem(row // cores, inner)
    a = row // (cores * inner)

    def index(a_, b_, c_):
        return (a_ * inner + b_) * cores + c_

    a_peers = [lax.rem(a + k, outer) for k in range(1, outer)]
    b_peers = [lax.rem(b + k, inner) for k in range(1, inner)]
    c_peers = [lax.rem(c + k, cores) for k in range(1, cores)]
    col_peers = [lax.rem(col + k, n_col) for k in range(1, n_col)]

    barrier = pltpu.get_barrier_semaphore()
    partners = [(index(p, b, c), col) for p in a_peers]
    partners += [(index(a, p, c), col) for p in b_peers]
    partners += [(index(a, b, p), col) for p in c_peers]
    partners += [(row, p) for p in col_peers]
    for partner in partners:
        pl.semaphore_signal(barrier, inc=1, device_id=partner, device_id_type=MESH)

    pairs = [
        (pivot_hbm, g_blocks.at[row]),
        (top_hbm, top),
        (right_hbm, right),
        (col_ranks_hbm, col_ranks),
        (row_ranks_hbm, row_ranks),
        (bases_hbm, bases),
        (left_hbm, left),
        (inverse_hbm, inverse),
    ]
    loads = [
        pltpu.make_async_copy(source, target, load_sem.at[number])
        for number, (source, target) in enumerate(pairs)
    ]
    for load in loads:
        load.start()

    def sender(blocks, send_sems, recv_sems):
        started = []

        def send(which, target):
            copy = pltpu.make_async_remote_copy(
                src_ref=blocks.at[which],
                dst_ref=blocks.at[which],
                send_sem=send_sems.at[len(started)],
                recv_sem=recv_sems.at[which],
                device_id=(target, col),
                device_id_type=MESH,
            )
            copy.start()
            started.append(copy)

        def arrived(which):
            pltpu.make_async_copy(blocks.at[which], blocks.at[which], recv_sems.at[which]).wait()

        return started, send, arrived

    g_started, g_move, g_arrived = sender(g_blocks, g_send, g_recv)
    m_started, m_move, m_arrived = sender(m_blocks, m_send, m_recv)

    def send_own(move):
        for p in reversed(a_peers):
            move(row, index(p, b, c))
        for p in b_peers:
            move(row, index(a, p, c))
        for p in c_peers:
            move(row, index(a, b, p))

    def from_outer(p, move, landed):
        s = index(p, b, c)
        landed(s)
        for q in b_peers:
            move(s, index(a, q, c))
        for q in c_peers:
            move(s, index(a, b, q))

    def from_inner(a_, move, landed):
        for p in b_peers:
            s = index(a_, p, c)
            landed(s)
            for q in c_peers:
                move(s, index(a, b, q))

    def from_cores(landed):
        for q in c_peers:
            for p in [a] + a_peers:
                for r in [b] + b_peers:
                    landed(index(p, r, q))

    loads[0].wait()
    pl.semaphore_wait(barrier, len(partners))
    send_own(g_move)

    for load in loads[1:5]:
        load.wait()
    levels = lax.broadcasted_iota(jnp.int32, (1, rank), 1)
    for j in range(m_tiles):
        part = jnp.dot(
            top[:, j * order : (j + 1) * order],
            right[j * order : (j + 1) * order, :],
            preferred_element_type=jnp.float32,
        )
        part = jnp.where(levels < col_ranks[j], part, 0.0)
        m_blocks[row, :, j * rank : (j + 1) * rank] = part.astype(jnp.bfloat16)
    send_own(m_move)

    for p in a_peers:
        from_outer(p, g_move, g_arrived)

    for load in loads[5:]:
        load.wait()
    rows = lax.broadcasted_iota(jnp.int32, (rank, 1), 0)
    for i in range(n_tiles):
        part = lax.dot_general(
            bases[i * order : (i + 1) * order, :],
            left[i * order : (i + 1) * order, :],
            (((0,), (0,)), ((), ())),
            preferred_element_type=jnp.float32,
        )
        part = jnp.where(rows < row_ranks[i], part, 0.0)
        cores_k[col, i] = part.astype(jnp.bfloat16)
    k_copies = []
    for number, p in enumerate(col_peers):
        copy = pltpu.make_async_remote_copy(
            src_ref=cores_k.at[col],
            dst_ref=cores_k.at[col],
            send_sem=k_send.at[number],
            recv_sem=k_recv.at[col],
            device_id=(row, p),
            device_id_type=MESH,
        )
        copy.start()
        k_copies.append(copy)

    previous = a
    for p in a_peers:
        from_inner(previous, g_move, g_arrived)
        from_outer(p, m_move, m_arrived)
        from_inner(previous, m_move, m_arrived)
        previous = p
    from_inner(previous, g_move, g_arrived)
    from_inner(previous, m_move, m_arrived)

    from_cores(g_arrived)
    solved = jnp.dot(
        inverse[...],
        g_blocks[...].reshape(order, g_blocks.shape[2]),
        preferred_element_type=jnp.float32,
    ).astype(jnp.bfloat16)
    for p in col_peers:
        pltpu.make_async_copy(cores_k.at[p], cores_k.at[p], k_recv.at[p]).wait()
    for i in range(n_tiles):
        total = jnp.zeros((rank, solved.shape[1]), jnp.float32)
        for k in range(n_col):
            total += jnp.dot(
                cores_k[k, i],
                solved[k * width : (k + 1) * width],
                preferred_element_type=jnp.float32,
            )
        reduced_out[i] = total.astype(jnp.bfloat16)

    from_cores(m_arrived)
    depth, m_width = m_blocks.shape[1:]
    share = n_row // n_col
    for i in range(n_tiles):
        total = jnp.zeros((rank, m_width), jnp.float32)
        for k in range(n_col):
            piece = m_blocks[k * share : (k + 1) * share]
            total += jnp.dot(
                cores_k[k, i],
                piece.reshape(share * depth, m_width),
                preferred_element_type=jnp.float32,
            )
        core_out[i] = total.astype(jnp.bfloat16)

    for copy in g_started + m_started + k_copies:
        copy.wait_send()


def update_kernel(
    core,
    reduced,
    bases_hbm,
    right_hbm,
    slab_hbm,
    rhs_hbm,
    slab_out_hbm,
    rhs_out_hbm,
    bases,
    right,
    slab,
    rhs,
    slab_out,
    rhs_out,
    load_sem,
    in_sem,
    out_sem,
):
    n_tiles, rank, wide = core.shape
    m_tiles = wide // rank
    order = bases.shape[0] // n_tiles
    chunks = [
        (pl.ds(i * order, order), pl.ds(j * order, order))
        for i in range(n_tiles)
        for j in range(m_tiles)
    ]
    first = [
        pltpu.make_async_copy(bases_hbm, bases, load_sem.at[0]),
        pltpu.make_async_copy(right_hbm, right, load_sem.at[1]),
    ]
    later = pltpu.make_async_copy(rhs_hbm, rhs, load_sem.at[2])
    loads = [
        pltpu.make_async_copy(slab_hbm.at[at], slab.at[at], in_sem.at[number])
        for number, at in enumerate(chunks)
    ]
    stores = [
        pltpu.make_async_copy(slab_out.at[at], slab_out_hbm.at[at], out_sem.at[number])
        for number, at in enumerate(chunks)
    ]
    for load in first + loads + [later]:
        load.start()
    for load in first:
        load.wait()
    for number, (at_row, at_col) in enumerate(chunks):
        i, j = number // m_tiles, number % m_tiles
        spread = jnp.dot(
            bases[at_row, :],
            core[i, :, j * rank : (j + 1) * rank],
            preferred_element_type=jnp.float32,
        ).astype(jnp.bfloat16)
        change = lax.dot_general(
            spread,
            right[at_col, :],
            (((1,), (1,)), ((), ())),
            preferred_element_type=jnp.float32,
        )
        loads[number].wait()
        slab_out[at_row, at_col] = (slab[at_row, at_col].astype(jnp.float32) - change).astype(
            jnp.bfloat16
        )
        stores[number].start()
    later.wait()
    for i in range(n_tiles):
        at = pl.ds(i * order, order)
        lowered = jnp.dot(bases[at, :], reduced[i], preferred_element_type=jnp.float32)
        rhs_out[at, :] = (rhs[at, :].astype(jnp.float32) - lowered).astype(jnp.bfloat16)
        store = pltpu.make_async_copy(
            rhs_out.at[at], rhs_out_hbm.at[at], out_sem.at[len(chunks) + i]
        )
        store.start()
        stores.append(store)
    for store in stores:
        store.wait()


def per_device(
    n_row,
    n_col,
    slab,
    panel_left,
    panel_top,
    row_bases,
    col_bases,
    row_ranks,
    col_ranks,
    pivot_inverse,
    pivot_rhs,
    rhs,
):
    order = pivot_inverse.shape[0]
    rank = row_bases.shape[1]
    n_tiles = row_ranks.shape[0]
    m_tiles = col_ranks.shape[0]
    gains = rhs.shape[1]
    width = panel_left.shape[1]
    outer, inner, cores = grid_of(n_row)
    sends = (outer - 1) + outer * (inner - 1) + outer * inner * (cores - 1)
    vmem = pl.BlockSpec(memory_space=pltpu.VMEM)
    hbm = pl.BlockSpec(memory_space=pltpu.HBM)
    core, reduced = pl.pallas_call(
        functools.partial(gather_kernel, n_row, n_col),
        out_shape=(
            jax.ShapeDtypeStruct((n_tiles, rank, m_tiles * rank), jnp.bfloat16),
            jax.ShapeDtypeStruct((n_tiles, rank, gains), jnp.bfloat16),
        ),
        in_specs=[hbm] * 8,
        out_specs=(vmem, vmem),
        scratch_shapes=[
            pltpu.SMEM(col_ranks.shape, col_ranks.dtype),
            pltpu.SMEM(row_ranks.shape, row_ranks.dtype),
            pltpu.VMEM(panel_top.shape, jnp.bfloat16),
            pltpu.VMEM(col_bases.shape, jnp.bfloat16),
            pltpu.VMEM(panel_left.shape, jnp.bfloat16),
            pltpu.VMEM(row_bases.shape, jnp.bfloat16),
            pltpu.VMEM(pivot_inverse.shape, jnp.bfloat16),
            pltpu.VMEM((n_row, panel_top.shape[0], m_tiles * rank), jnp.bfloat16),
            pltpu.VMEM((n_row, pivot_rhs.shape[0], gains), jnp.bfloat16),
            pltpu.VMEM((n_col, n_tiles, rank, width), jnp.bfloat16),
            pltpu.SemaphoreType.DMA((8,)),
            pltpu.SemaphoreType.DMA((sends,)),
            pltpu.SemaphoreType.DMA((n_row,)),
            pltpu.SemaphoreType.DMA((sends,)),
            pltpu.SemaphoreType.DMA((n_row,)),
            pltpu.SemaphoreType.DMA((max(n_col - 1, 1),)),
            pltpu.SemaphoreType.DMA((n_col,)),
        ],
        compiler_params=pltpu.CompilerParams(
            collective_id=0, has_side_effects=True, vmem_limit_bytes=62 * 2**20
        ),
        name="gather",
    )(col_ranks, row_ranks, panel_top, col_bases, panel_left, row_bases, pivot_inverse, pivot_rhs)

    return pl.pallas_call(
        update_kernel,
        out_shape=(
            jax.ShapeDtypeStruct(slab.shape, slab.dtype),
            jax.ShapeDtypeStruct(rhs.shape, rhs.dtype),
        ),
        in_specs=[vmem] * 2 + [hbm] * 4,
        out_specs=(hbm, hbm),
        scratch_shapes=[
            pltpu.VMEM(row_bases.shape, jnp.bfloat16),
            pltpu.VMEM(col_bases.shape, jnp.bfloat16),
            pltpu.VMEM(slab.shape, jnp.bfloat16),
            pltpu.VMEM(rhs.shape, jnp.bfloat16),
            pltpu.VMEM(slab.shape, jnp.bfloat16),
            pltpu.VMEM(rhs.shape, jnp.bfloat16),
            pltpu.SemaphoreType.DMA((3,)),
            pltpu.SemaphoreType.DMA((n_tiles * m_tiles,)),
            pltpu.SemaphoreType.DMA((n_tiles * m_tiles + n_tiles,)),
        ],
        compiler_params=pltpu.CompilerParams(vmem_limit_bytes=62 * 2**20),
        name="update",
    )(core, reduced, row_bases, col_bases, slab, rhs)


def solution(mesh):
    in_specs = (
        P("row", "col"),
        P("row", "col"),
        P("row", "col"),
        P("row", None),
        P("col", None),
        P("row"),
        P("col"),
        P(),
        P("row", "col"),
        P("row", "col"),
    )
    out_specs = (P("row", "col"), P("row", "col"))
    return jax.shard_map(
        functools.partial(per_device, mesh.shape["row"], mesh.shape["col"]),
        mesh=mesh,
        in_specs=in_specs,
        out_specs=out_specs,
        check_vma=False,
    )
```

```python
import functools

import jax
import jax.numpy as jnp
from jax import lax
from jax.experimental import pallas as pl
from jax.experimental.pallas import tpu as pltpu
from jax.sharding import PartitionSpec as P

MESH = pl.DeviceIdType.MESH


def grid_of(count):
    cores = 2 if count % 2 == 0 else 1
    chips = count // cores
    inner = max(d for d in range(1, chips + 1) if chips % d == 0 and d * d <= chips)
    return chips // inner, inner, cores


def gather_kernel(
    n_row,
    n_col,
    col_ranks_hbm,
    row_ranks_hbm,
    top_hbm,
    right_hbm,
    left_hbm,
    bases_hbm,
    inverse_hbm,
    pivot_hbm,
    core_out,
    reduced_out,
    col_ranks,
    row_ranks,
    top,
    right,
    left,
    bases,
    inverse,
    m_blocks,
    g_blocks,
    cores_k,
    load_sem,
    m_send,
    m_recv,
    g_send,
    g_recv,
    k_send,
    k_recv,
):
    outer, inner, cores = grid_of(n_row)
    order = inverse.shape[0]
    rank = bases.shape[1]
    n_tiles = row_ranks.shape[0]
    m_tiles = col_ranks.shape[0]
    width = left.shape[1]

    row = lax.axis_index("row")
    col = lax.axis_index("col")
    c = lax.rem(row, cores)
    b = lax.rem(row // cores, inner)
    a = row // (cores * inner)

    def index(a_, b_, c_):
        return (a_ * inner + b_) * cores + c_

    a_peers = [lax.rem(a + k, outer) for k in range(1, outer)]
    b_peers = [lax.rem(b + k, inner) for k in range(1, inner)]
    c_peers = [lax.rem(c + k, cores) for k in range(1, cores)]
    col_peers = [lax.rem(col + k, n_col) for k in range(1, n_col)]

    barrier = pltpu.get_barrier_semaphore()
    partners = [(index(p, b, c), col) for p in a_peers]
    partners += [(index(a, p, c), col) for p in b_peers]
    partners += [(index(a, b, p), col) for p in c_peers]
    partners += [(row, p) for p in col_peers]
    for partner in partners:
        pl.semaphore_signal(barrier, inc=1, device_id=partner, device_id_type=MESH)

    pairs = [
        (pivot_hbm, g_blocks.at[row]),
        (top_hbm, top),
        (right_hbm, right),
        (col_ranks_hbm, col_ranks),
        (row_ranks_hbm, row_ranks),
        (bases_hbm, bases),
        (left_hbm, left),
        (inverse_hbm, inverse),
    ]
    loads = [
        pltpu.make_async_copy(source, target, load_sem.at[number])
        for number, (source, target) in enumerate(pairs)
    ]
    for load in loads:
        load.start()

    steps = [(k, way) for k in range(1, outer) for way in (1, -1)]

    def inside(p):
        return jnp.logical_and(p >= 0, p < outer)

    def always(action):
        action()

    def sender(blocks, send_sems, recv_sems):
        started = []

        def send(which, target, when):
            copy = pltpu.make_async_remote_copy(
                src_ref=blocks.at[which],
                dst_ref=blocks.at[which],
                send_sem=send_sems.at[len(started)],
                recv_sem=recv_sems.at[which],
                device_id=(target, col),
                device_id_type=MESH,
            )
            when(copy.start)
            started.append((copy, when))

        def arrived(which, when):
            when(
                pltpu.make_async_copy(blocks.at[which], blocks.at[which], recv_sems.at[which]).wait
            )

        return started, send, arrived

    g_started, g_move, g_arrived = sender(g_blocks, g_send, g_recv)
    m_started, m_move, m_arrived = sender(m_blocks, m_send, m_recv)

    def send_own(move):
        for way in (1, -1):
            move(row, index(a + way, b, c), pl.when(inside(a + way)))
        for p in b_peers:
            move(row, index(a, p, c), always)
        for p in c_peers:
            move(row, index(a, b, p), always)

    def from_outer(k, way, move, landed):
        when = pl.when(inside(a - way * k))
        s = index(a - way * k, b, c)
        landed(s, when)
        if k < outer - 1:
            move(
                s,
                index(a + way, b, c),
                pl.when(jnp.logical_and(inside(a - way * k), inside(a + way))),
            )
        for q in b_peers:
            move(s, index(a, q, c), when)
        for q in c_peers:
            move(s, index(a, b, q), when)

    def from_inner(k, way, move, landed):
        when = pl.when(inside(a - way * k)) if k else always
        for p in b_peers:
            s = index(a - way * k, p, c)
            landed(s, when)
            for q in c_peers:
                move(s, index(a, b, q), when)

    def from_cores(landed):
        for q in c_peers:
            for p in range(outer):
                for r in range(inner):
                    landed(index(p, r, q), always)

    loads[0].wait()
    pl.semaphore_wait(barrier, len(partners))
    send_own(g_move)

    for load in loads[1:5]:
        load.wait()
    levels = lax.broadcasted_iota(jnp.int32, (1, rank), 1)
    for j in range(m_tiles):
        part = jnp.dot(
            top[:, j * order : (j + 1) * order],
            right[j * order : (j + 1) * order, :],
            preferred_element_type=jnp.float32,
        )
        part = jnp.where(levels < col_ranks[j], part, 0.0)
        m_blocks[row, :, j * rank : (j + 1) * rank] = part.astype(jnp.bfloat16)
    send_own(m_move)

    for k, way in steps[:2]:
        from_outer(k, way, g_move, g_arrived)

    for load in loads[5:]:
        load.wait()
    rows = lax.broadcasted_iota(jnp.int32, (rank, 1), 0)
    for i in range(n_tiles):
        part = lax.dot_general(
            bases[i * order : (i + 1) * order, :],
            left[i * order : (i + 1) * order, :],
            (((0,), (0,)), ((), ())),
            preferred_element_type=jnp.float32,
        )
        part = jnp.where(rows < row_ranks[i], part, 0.0)
        cores_k[col, i] = part.astype(jnp.bfloat16)
    k_copies = []
    for number, p in enumerate(col_peers):
        copy = pltpu.make_async_remote_copy(
            src_ref=cores_k.at[col],
            dst_ref=cores_k.at[col],
            send_sem=k_send.at[number],
            recv_sem=k_recv.at[col],
            device_id=(row, p),
            device_id_type=MESH,
        )
        copy.start()
        k_copies.append(copy)

    from_inner(0, 1, g_move, g_arrived)
    for k, way in steps[2:4]:
        from_outer(k, way, g_move, g_arrived)
    for k, way in steps[:2]:
        from_outer(k, way, m_move, m_arrived)
        from_inner(k, way, g_move, g_arrived)
    from_inner(0, 1, m_move, m_arrived)
    for k, way in steps[4:]:
        from_outer(k, way, g_move, g_arrived)
    for number, (k, way) in enumerate(steps[2:]):
        from_outer(k, way, m_move, m_arrived)
        from_inner(k, way, g_move, g_arrived)
        from_inner(*steps[number], m_move, m_arrived)
    for k, way in steps[-2:]:
        from_inner(k, way, m_move, m_arrived)

    from_cores(g_arrived)
    solved = jnp.dot(
        inverse[...],
        g_blocks[...].reshape(order, g_blocks.shape[2]),
        preferred_element_type=jnp.float32,
    ).astype(jnp.bfloat16)
    for p in col_peers:
        pltpu.make_async_copy(cores_k.at[p], cores_k.at[p], k_recv.at[p]).wait()
    for i in range(n_tiles):
        total = jnp.zeros((rank, solved.shape[1]), jnp.float32)
        for k in range(n_col):
            total += jnp.dot(
                cores_k[k, i],
                solved[k * width : (k + 1) * width],
                preferred_element_type=jnp.float32,
            )
        reduced_out[i] = total.astype(jnp.bfloat16)

    from_cores(m_arrived)
    depth, m_width = m_blocks.shape[1:]
    share = n_row // n_col
    for i in range(n_tiles):
        total = jnp.zeros((rank, m_width), jnp.float32)
        for k in range(n_col):
            piece = m_blocks[k * share : (k + 1) * share]
            total += jnp.dot(
                cores_k[k, i],
                piece.reshape(share * depth, m_width),
                preferred_element_type=jnp.float32,
            )
        core_out[i] = total.astype(jnp.bfloat16)

    for copy, when in g_started + m_started:
        when(copy.wait_send)
    for copy in k_copies:
        copy.wait_send()


def update_kernel(
    core_hbm,
    reduced_hbm,
    bases_hbm,
    right_hbm,
    slab_hbm,
    rhs_hbm,
    slab_out_hbm,
    rhs_out_hbm,
    core,
    reduced,
    bases,
    right,
    slab,
    rhs,
    slab_out,
    rhs_out,
    load_sem,
    in_sem,
    out_sem,
):
    n_tiles, rank, wide = core.shape
    m_tiles = wide // rank
    order = bases.shape[0] // n_tiles
    chunks = [
        (pl.ds(i * order, order), pl.ds(j * order, order))
        for i in range(n_tiles)
        for j in range(m_tiles)
    ]
    first = [
        pltpu.make_async_copy(core_hbm, core, load_sem.at[3]),
        pltpu.make_async_copy(bases_hbm, bases, load_sem.at[0]),
        pltpu.make_async_copy(right_hbm, right, load_sem.at[1]),
    ]
    later = [
        pltpu.make_async_copy(rhs_hbm, rhs, load_sem.at[2]),
        pltpu.make_async_copy(reduced_hbm, reduced, load_sem.at[4]),
    ]
    loads = [
        pltpu.make_async_copy(slab_hbm.at[at], slab.at[at], in_sem.at[number])
        for number, at in enumerate(chunks)
    ]
    stores = [
        pltpu.make_async_copy(slab_out.at[at], slab_out_hbm.at[at], out_sem.at[number])
        for number, at in enumerate(chunks)
    ]
    for load in first + loads + later:
        load.start()
    for load in first:
        load.wait()
    for number, (at_row, at_col) in enumerate(chunks):
        i, j = number // m_tiles, number % m_tiles
        spread = jnp.dot(
            bases[at_row, :],
            core[i, :, j * rank : (j + 1) * rank],
            preferred_element_type=jnp.float32,
        ).astype(jnp.bfloat16)
        change = lax.dot_general(
            spread,
            right[at_col, :],
            (((1,), (1,)), ((), ())),
            preferred_element_type=jnp.float32,
        )
        loads[number].wait()
        slab_out[at_row, at_col] = (slab[at_row, at_col].astype(jnp.float32) - change).astype(
            jnp.bfloat16
        )
        stores[number].start()
    for load in later:
        load.wait()
    for i in range(n_tiles):
        at = pl.ds(i * order, order)
        lowered = jnp.dot(bases[at, :], reduced[i], preferred_element_type=jnp.float32)
        rhs_out[at, :] = (rhs[at, :].astype(jnp.float32) - lowered).astype(jnp.bfloat16)
        store = pltpu.make_async_copy(
            rhs_out.at[at], rhs_out_hbm.at[at], out_sem.at[len(chunks) + i]
        )
        store.start()
        stores.append(store)
    for store in stores:
        store.wait()


def per_device(
    n_row,
    n_col,
    slab,
    panel_left,
    panel_top,
    row_bases,
    col_bases,
    row_ranks,
    col_ranks,
    pivot_inverse,
    pivot_rhs,
    rhs,
):
    order = pivot_inverse.shape[0]
    rank = row_bases.shape[1]
    n_tiles = row_ranks.shape[0]
    m_tiles = col_ranks.shape[0]
    gains = rhs.shape[1]
    width = panel_left.shape[1]
    outer, inner, cores = grid_of(n_row)
    slots = 2 * outer - 1
    sends = 2 * (outer - 1) + slots * (inner - 1) + slots * inner * (cores - 1)
    vmem = pl.BlockSpec(memory_space=pltpu.VMEM)
    hbm = pl.BlockSpec(memory_space=pltpu.HBM)
    core, reduced = pl.pallas_call(
        functools.partial(gather_kernel, n_row, n_col),
        out_shape=(
            jax.ShapeDtypeStruct((n_tiles, rank, m_tiles * rank), jnp.bfloat16),
            jax.ShapeDtypeStruct((n_tiles, rank, gains), jnp.bfloat16),
        ),
        in_specs=[hbm] * 8,
        out_specs=(vmem, vmem),
        scratch_shapes=[
            pltpu.SMEM(col_ranks.shape, col_ranks.dtype),
            pltpu.SMEM(row_ranks.shape, row_ranks.dtype),
            pltpu.VMEM(panel_top.shape, jnp.bfloat16),
            pltpu.VMEM(col_bases.shape, jnp.bfloat16),
            pltpu.VMEM(panel_left.shape, jnp.bfloat16),
            pltpu.VMEM(row_bases.shape, jnp.bfloat16),
            pltpu.VMEM(pivot_inverse.shape, jnp.bfloat16),
            pltpu.VMEM((n_row, panel_top.shape[0], m_tiles * rank), jnp.bfloat16),
            pltpu.VMEM((n_row, pivot_rhs.shape[0], gains), jnp.bfloat16),
            pltpu.VMEM((n_col, n_tiles, rank, width), jnp.bfloat16),
            pltpu.SemaphoreType.DMA((8,)),
            pltpu.SemaphoreType.DMA((sends,)),
            pltpu.SemaphoreType.DMA((n_row,)),
            pltpu.SemaphoreType.DMA((sends,)),
            pltpu.SemaphoreType.DMA((n_row,)),
            pltpu.SemaphoreType.DMA((max(n_col - 1, 1),)),
            pltpu.SemaphoreType.DMA((n_col,)),
        ],
        compiler_params=pltpu.CompilerParams(
            collective_id=0, has_side_effects=True, vmem_limit_bytes=62 * 2**20
        ),
        name="gather",
    )(col_ranks, row_ranks, panel_top, col_bases, panel_left, row_bases, pivot_inverse, pivot_rhs)

    return pl.pallas_call(
        update_kernel,
        out_shape=(
            jax.ShapeDtypeStruct(slab.shape, slab.dtype),
            jax.ShapeDtypeStruct(rhs.shape, rhs.dtype),
        ),
        in_specs=[hbm] * 6,
        out_specs=(hbm, hbm),
        scratch_shapes=[
            pltpu.VMEM(core.shape, jnp.bfloat16),
            pltpu.VMEM(reduced.shape, jnp.bfloat16),
            pltpu.VMEM(row_bases.shape, jnp.bfloat16),
            pltpu.VMEM(col_bases.shape, jnp.bfloat16),
            pltpu.VMEM(slab.shape, jnp.bfloat16),
            pltpu.VMEM(rhs.shape, jnp.bfloat16),
            pltpu.VMEM(slab.shape, jnp.bfloat16),
            pltpu.VMEM(rhs.shape, jnp.bfloat16),
            pltpu.SemaphoreType.DMA((5,)),
            pltpu.SemaphoreType.DMA((n_tiles * m_tiles,)),
            pltpu.SemaphoreType.DMA((n_tiles * m_tiles + n_tiles,)),
        ],
        compiler_params=pltpu.CompilerParams(vmem_limit_bytes=62 * 2**20),
        name="update",
    )(core, reduced, row_bases, col_bases, slab, rhs)


def solution(mesh):
    in_specs = (
        P("row", "col"),
        P("row", "col"),
        P("row", "col"),
        P("row", None),
        P("col", None),
        P("row"),
        P("col"),
        P(),
        P("row", "col"),
        P("row", "col"),
    )
    out_specs = (P("row", "col"), P("row", "col"))
    return jax.shard_map(
        functools.partial(per_device, mesh.shape["row"], mesh.shape["col"]),
        mesh=mesh,
        in_specs=in_specs,
        out_specs=out_specs,
        check_vma=False,
    )
```

```python
import functools

import jax
import jax.numpy as jnp
from jax import lax
from jax.experimental import pallas as pl
from jax.experimental.pallas import tpu as pltpu
from jax.sharding import PartitionSpec as P

MESH = pl.DeviceIdType.MESH


def grid_of(count):
    cores = 2 if count % 2 == 0 else 1
    chips = count // cores
    inner = max(d for d in range(1, chips + 1) if chips % d == 0 and d * d <= chips)
    return chips // inner, inner, cores


def gather_kernel(
    n_row,
    n_col,
    col_ranks_hbm,
    row_ranks_hbm,
    top_hbm,
    right_hbm,
    left_hbm,
    bases_hbm,
    inverse_hbm,
    pivot_hbm,
    core_out,
    reduced_out,
    col_ranks,
    row_ranks,
    top,
    right,
    left,
    bases,
    inverse,
    m_blocks,
    g_blocks,
    cores_k,
    load_sem,
    m_send,
    m_recv,
    g_send,
    g_recv,
    k_send,
    k_recv,
):
    outer, inner, cores = grid_of(n_row)
    order = inverse.shape[0]
    rank = bases.shape[1]
    n_tiles = row_ranks.shape[0]
    m_tiles = col_ranks.shape[0]
    width = left.shape[1]

    row = lax.axis_index("row")
    col = lax.axis_index("col")
    c = lax.rem(row, cores)
    b = lax.rem(row // cores, inner)
    a = row // (cores * inner)

    def index(a_, b_, c_):
        return (a_ * inner + b_) * cores + c_

    a_peers = [lax.rem(a + k, outer) for k in range(1, outer)]
    b_peers = [lax.rem(b + k, inner) for k in range(1, inner)]
    c_peers = [lax.rem(c + k, cores) for k in range(1, cores)]
    col_peers = [lax.rem(col + k, n_col) for k in range(1, n_col)]

    barrier = pltpu.get_barrier_semaphore()
    partners = [(index(p, b, c), col) for p in a_peers]
    partners += [(index(a, p, c), col) for p in b_peers]
    partners += [(index(a, b, p), col) for p in c_peers]
    partners += [(row, p) for p in col_peers]
    for partner in partners:
        pl.semaphore_signal(barrier, inc=1, device_id=partner, device_id_type=MESH)

    pairs = [
        (pivot_hbm, g_blocks.at[row]),
        (top_hbm, top),
        (right_hbm, right),
        (col_ranks_hbm, col_ranks),
        (row_ranks_hbm, row_ranks),
        (bases_hbm, bases),
        (left_hbm, left),
        (inverse_hbm, inverse),
    ]
    loads = [
        pltpu.make_async_copy(source, target, load_sem.at[number])
        for number, (source, target) in enumerate(pairs)
    ]
    for load in loads:
        load.start()

    steps = [(k, way) for k in range(1, outer) for way in (1, -1)]

    def inside(p):
        return jnp.logical_and(p >= 0, p < outer)

    def always(action):
        action()

    def sender(blocks, send_sems, recv_sems):
        started = []

        def send(which, target, when):
            copy = pltpu.make_async_remote_copy(
                src_ref=blocks.at[which],
                dst_ref=blocks.at[which],
                send_sem=send_sems.at[len(started)],
                recv_sem=recv_sems.at[which],
                device_id=(target, col),
                device_id_type=MESH,
            )
            when(copy.start)
            started.append((copy, when))

        def arrived(which, when):
            when(
                pltpu.make_async_copy(blocks.at[which], blocks.at[which], recv_sems.at[which]).wait
            )

        return started, send, arrived

    g_started, g_move, g_arrived = sender(g_blocks, g_send, g_recv)
    m_started, m_move, m_arrived = sender(m_blocks, m_send, m_recv)

    def send_own(move):
        for k, way in steps:
            move(row, index(a + way * k, b, c), pl.when(inside(a + way * k)))
        for p in b_peers:
            move(row, index(a, p, c), always)
        for p in c_peers:
            move(row, index(a, b, p), always)

    def from_outer(k, way, move, landed):
        when = pl.when(inside(a - way * k))
        s = index(a - way * k, b, c)
        landed(s, when)
        for q in b_peers:
            move(s, index(a, q, c), when)
        for q in c_peers:
            move(s, index(a, b, q), when)

    def from_inner(k, way, move, landed):
        when = pl.when(inside(a - way * k)) if k else always
        for p in b_peers:
            s = index(a - way * k, p, c)
            landed(s, when)
            for q in c_peers:
                move(s, index(a, b, q), when)

    def from_cores(landed):
        for q in c_peers:
            for p in range(outer):
                for r in range(inner):
                    landed(index(p, r, q), always)

    loads[0].wait()
    pl.semaphore_wait(barrier, len(partners))
    send_own(g_move)

    for load in loads[1:5]:
        load.wait()
    levels = lax.broadcasted_iota(jnp.int32, (1, rank), 1)
    for j in range(m_tiles):
        part = jnp.dot(
            top[:, j * order : (j + 1) * order],
            right[j * order : (j + 1) * order, :],
            preferred_element_type=jnp.float32,
        )
        part = jnp.where(levels < col_ranks[j], part, 0.0)
        m_blocks[row, :, j * rank : (j + 1) * rank] = part.astype(jnp.bfloat16)
    send_own(m_move)

    for k, way in steps[:2]:
        from_outer(k, way, g_move, g_arrived)

    for load in loads[5:]:
        load.wait()
    rows = lax.broadcasted_iota(jnp.int32, (rank, 1), 0)
    for i in range(n_tiles):
        part = lax.dot_general(
            bases[i * order : (i + 1) * order, :],
            left[i * order : (i + 1) * order, :],
            (((0,), (0,)), ((), ())),
            preferred_element_type=jnp.float32,
        )
        part = jnp.where(rows < row_ranks[i], part, 0.0)
        cores_k[col, i] = part.astype(jnp.bfloat16)
    k_copies = []
    for number, p in enumerate(col_peers):
        copy = pltpu.make_async_remote_copy(
            src_ref=cores_k.at[col],
            dst_ref=cores_k.at[col],
            send_sem=k_send.at[number],
            recv_sem=k_recv.at[col],
            device_id=(row, p),
            device_id_type=MESH,
        )
        copy.start()
        k_copies.append(copy)

    from_inner(0, 1, g_move, g_arrived)
    for k, way in steps[2:4]:
        from_outer(k, way, g_move, g_arrived)
    for k, way in steps[:2]:
        from_outer(k, way, m_move, m_arrived)
        from_inner(k, way, g_move, g_arrived)
    from_inner(0, 1, m_move, m_arrived)
    for k, way in steps[4:]:
        from_outer(k, way, g_move, g_arrived)
    for number, (k, way) in enumerate(steps[2:]):
        from_outer(k, way, m_move, m_arrived)
        from_inner(k, way, g_move, g_arrived)
        from_inner(*steps[number], m_move, m_arrived)
    for k, way in steps[-2:]:
        from_inner(k, way, m_move, m_arrived)

    from_cores(g_arrived)
    solved = jnp.dot(
        inverse[...],
        g_blocks[...].reshape(order, g_blocks.shape[2]),
        preferred_element_type=jnp.float32,
    ).astype(jnp.bfloat16)
    for p in col_peers:
        pltpu.make_async_copy(cores_k.at[p], cores_k.at[p], k_recv.at[p]).wait()
    for i in range(n_tiles):
        total = jnp.zeros((rank, solved.shape[1]), jnp.float32)
        for k in range(n_col):
            total += jnp.dot(
                cores_k[k, i],
                solved[k * width : (k + 1) * width],
                preferred_element_type=jnp.float32,
            )
        reduced_out[i] = total.astype(jnp.bfloat16)

    from_cores(m_arrived)
    depth, m_width = m_blocks.shape[1:]
    share = n_row // n_col
    for i in range(n_tiles):
        total = jnp.zeros((rank, m_width), jnp.float32)
        for k in range(n_col):
            piece = m_blocks[k * share : (k + 1) * share]
            total += jnp.dot(
                cores_k[k, i],
                piece.reshape(share * depth, m_width),
                preferred_element_type=jnp.float32,
            )
        core_out[i] = total.astype(jnp.bfloat16)

    for copy, when in g_started + m_started:
        when(copy.wait_send)
    for copy in k_copies:
        copy.wait_send()


def update_kernel(
    core_hbm,
    reduced_hbm,
    bases_hbm,
    right_hbm,
    slab_hbm,
    rhs_hbm,
    slab_out_hbm,
    rhs_out_hbm,
    core,
    reduced,
    bases,
    right,
    slab,
    rhs,
    slab_out,
    rhs_out,
    load_sem,
    in_sem,
    out_sem,
):
    n_tiles, rank, wide = core.shape
    m_tiles = wide // rank
    order = bases.shape[0] // n_tiles
    chunks = [
        (pl.ds(i * order, order), pl.ds(j * order, order))
        for i in range(n_tiles)
        for j in range(m_tiles)
    ]
    first = [
        pltpu.make_async_copy(core_hbm, core, load_sem.at[3]),
        pltpu.make_async_copy(bases_hbm, bases, load_sem.at[0]),
        pltpu.make_async_copy(right_hbm, right, load_sem.at[1]),
    ]
    later = [
        pltpu.make_async_copy(rhs_hbm, rhs, load_sem.at[2]),
        pltpu.make_async_copy(reduced_hbm, reduced, load_sem.at[4]),
    ]
    loads = [
        pltpu.make_async_copy(slab_hbm.at[at], slab.at[at], in_sem.at[number])
        for number, at in enumerate(chunks)
    ]
    stores = [
        pltpu.make_async_copy(slab_out.at[at], slab_out_hbm.at[at], out_sem.at[number])
        for number, at in enumerate(chunks)
    ]
    for load in first + loads + later:
        load.start()
    for load in first:
        load.wait()
    for number, (at_row, at_col) in enumerate(chunks):
        i, j = number // m_tiles, number % m_tiles
        spread = jnp.dot(
            bases[at_row, :],
            core[i, :, j * rank : (j + 1) * rank],
            preferred_element_type=jnp.float32,
        ).astype(jnp.bfloat16)
        change = lax.dot_general(
            spread,
            right[at_col, :],
            (((1,), (1,)), ((), ())),
            preferred_element_type=jnp.float32,
        )
        loads[number].wait()
        slab_out[at_row, at_col] = (slab[at_row, at_col].astype(jnp.float32) - change).astype(
            jnp.bfloat16
        )
        stores[number].start()
    for load in later:
        load.wait()
    for i in range(n_tiles):
        at = pl.ds(i * order, order)
        lowered = jnp.dot(bases[at, :], reduced[i], preferred_element_type=jnp.float32)
        rhs_out[at, :] = (rhs[at, :].astype(jnp.float32) - lowered).astype(jnp.bfloat16)
        store = pltpu.make_async_copy(
            rhs_out.at[at], rhs_out_hbm.at[at], out_sem.at[len(chunks) + i]
        )
        store.start()
        stores.append(store)
    for store in stores:
        store.wait()


def per_device(
    n_row,
    n_col,
    slab,
    panel_left,
    panel_top,
    row_bases,
    col_bases,
    row_ranks,
    col_ranks,
    pivot_inverse,
    pivot_rhs,
    rhs,
):
    order = pivot_inverse.shape[0]
    rank = row_bases.shape[1]
    n_tiles = row_ranks.shape[0]
    m_tiles = col_ranks.shape[0]
    gains = rhs.shape[1]
    width = panel_left.shape[1]
    outer, inner, cores = grid_of(n_row)
    slots = 2 * outer - 1
    sends = 2 * (outer - 1) + slots * (inner - 1) + slots * inner * (cores - 1)
    vmem = pl.BlockSpec(memory_space=pltpu.VMEM)
    hbm = pl.BlockSpec(memory_space=pltpu.HBM)
    core, reduced = pl.pallas_call(
        functools.partial(gather_kernel, n_row, n_col),
        out_shape=(
            jax.ShapeDtypeStruct((n_tiles, rank, m_tiles * rank), jnp.bfloat16),
            jax.ShapeDtypeStruct((n_tiles, rank, gains), jnp.bfloat16),
        ),
        in_specs=[hbm] * 8,
        out_specs=(vmem, vmem),
        scratch_shapes=[
            pltpu.SMEM(col_ranks.shape, col_ranks.dtype),
            pltpu.SMEM(row_ranks.shape, row_ranks.dtype),
            pltpu.VMEM(panel_top.shape, jnp.bfloat16),
            pltpu.VMEM(col_bases.shape, jnp.bfloat16),
            pltpu.VMEM(panel_left.shape, jnp.bfloat16),
            pltpu.VMEM(row_bases.shape, jnp.bfloat16),
            pltpu.VMEM(pivot_inverse.shape, jnp.bfloat16),
            pltpu.VMEM((n_row, panel_top.shape[0], m_tiles * rank), jnp.bfloat16),
            pltpu.VMEM((n_row, pivot_rhs.shape[0], gains), jnp.bfloat16),
            pltpu.VMEM((n_col, n_tiles, rank, width), jnp.bfloat16),
            pltpu.SemaphoreType.DMA((8,)),
            pltpu.SemaphoreType.DMA((sends,)),
            pltpu.SemaphoreType.DMA((n_row,)),
            pltpu.SemaphoreType.DMA((sends,)),
            pltpu.SemaphoreType.DMA((n_row,)),
            pltpu.SemaphoreType.DMA((max(n_col - 1, 1),)),
            pltpu.SemaphoreType.DMA((n_col,)),
        ],
        compiler_params=pltpu.CompilerParams(
            collective_id=0, has_side_effects=True, vmem_limit_bytes=62 * 2**20
        ),
        name="gather",
    )(col_ranks, row_ranks, panel_top, col_bases, panel_left, row_bases, pivot_inverse, pivot_rhs)

    return pl.pallas_call(
        update_kernel,
        out_shape=(
            jax.ShapeDtypeStruct(slab.shape, slab.dtype),
            jax.ShapeDtypeStruct(rhs.shape, rhs.dtype),
        ),
        in_specs=[hbm] * 6,
        out_specs=(hbm, hbm),
        scratch_shapes=[
            pltpu.VMEM(core.shape, jnp.bfloat16),
            pltpu.VMEM(reduced.shape, jnp.bfloat16),
            pltpu.VMEM(row_bases.shape, jnp.bfloat16),
            pltpu.VMEM(col_bases.shape, jnp.bfloat16),
            pltpu.VMEM(slab.shape, jnp.bfloat16),
            pltpu.VMEM(rhs.shape, jnp.bfloat16),
            pltpu.VMEM(slab.shape, jnp.bfloat16),
            pltpu.VMEM(rhs.shape, jnp.bfloat16),
            pltpu.SemaphoreType.DMA((5,)),
            pltpu.SemaphoreType.DMA((n_tiles * m_tiles,)),
            pltpu.SemaphoreType.DMA((n_tiles * m_tiles + n_tiles,)),
        ],
        compiler_params=pltpu.CompilerParams(vmem_limit_bytes=62 * 2**20),
        name="update",
    )(core, reduced, row_bases, col_bases, slab, rhs)


def solution(mesh):
    in_specs = (
        P("row", "col"),
        P("row", "col"),
        P("row", "col"),
        P("row", None),
        P("col", None),
        P("row"),
        P("col"),
        P(),
        P("row", "col"),
        P("row", "col"),
    )
    out_specs = (P("row", "col"), P("row", "col"))
    return jax.shard_map(
        functools.partial(per_device, mesh.shape["row"], mesh.shape["col"]),
        mesh=mesh,
        in_specs=in_specs,
        out_specs=out_specs,
        check_vma=False,
    )
```

```python
import functools

import jax
import jax.numpy as jnp
from jax import lax
from jax.experimental import pallas as pl
from jax.experimental.pallas import tpu as pltpu
from jax.sharding import PartitionSpec as P

MESH = pl.DeviceIdType.MESH


def grid_of(count):
    cores = 2 if count % 2 == 0 else 1
    chips = count // cores
    inner = max(d for d in range(1, chips + 1) if chips % d == 0 and d * d <= chips)
    return chips // inner, inner, cores


def gather_kernel(
    n_row,
    n_col,
    col_ranks_hbm,
    row_ranks_hbm,
    top_hbm,
    right_hbm,
    left_hbm,
    bases_hbm,
    inverse_hbm,
    pivot_hbm,
    core_hbm,
    reduced_hbm,
    core_out,
    reduced_out,
    col_ranks,
    row_ranks,
    top,
    right,
    left,
    bases,
    inverse,
    m_blocks,
    g_blocks,
    cores_k,
    load_sem,
    store_sem,
    m_send,
    m_recv,
    g_send,
    g_recv,
    k_send,
    k_recv,
):
    outer, inner, cores = grid_of(n_row)
    order = inverse.shape[0]
    rank = bases.shape[1]
    n_tiles = row_ranks.shape[0]
    m_tiles = col_ranks.shape[0]
    width = left.shape[1]

    row = lax.axis_index("row")
    col = lax.axis_index("col")
    c = lax.rem(row, cores)
    b = lax.rem(row // cores, inner)
    a = row // (cores * inner)

    def index(a_, b_, c_):
        return (a_ * inner + b_) * cores + c_

    a_peers = [lax.rem(a + k, outer) for k in range(1, outer)]
    b_peers = [lax.rem(b + k, inner) for k in range(1, inner)]
    c_peers = [lax.rem(c + k, cores) for k in range(1, cores)]
    col_peers = [lax.rem(col + k, n_col) for k in range(1, n_col)]

    barrier = pltpu.get_barrier_semaphore()
    partners = [(index(p, b, c), col) for p in a_peers]
    partners += [(index(a, p, c), col) for p in b_peers]
    partners += [(index(a, b, p), col) for p in c_peers]
    partners += [(row, p) for p in col_peers]
    for partner in partners:
        pl.semaphore_signal(barrier, inc=1, device_id=partner, device_id_type=MESH)

    pairs = [
        (pivot_hbm, g_blocks.at[row]),
        (top_hbm, top),
        (right_hbm, right),
        (col_ranks_hbm, col_ranks),
        (row_ranks_hbm, row_ranks),
        (bases_hbm, bases),
        (left_hbm, left),
        (inverse_hbm, inverse),
    ]
    loads = [
        pltpu.make_async_copy(source, target, load_sem.at[number])
        for number, (source, target) in enumerate(pairs)
    ]
    for load in loads:
        load.start()

    steps = [(k, way) for k in range(1, outer) for way in (1, -1)]

    def inside(p):
        return jnp.logical_and(p >= 0, p < outer)

    def always(action):
        action()

    def sender(blocks, send_sems, recv_sems):
        started = []

        def send(which, target, when):
            copy = pltpu.make_async_remote_copy(
                src_ref=blocks.at[which],
                dst_ref=blocks.at[which],
                send_sem=send_sems.at[len(started)],
                recv_sem=recv_sems.at[which],
                device_id=(target, col),
                device_id_type=MESH,
            )
            when(copy.start)
            started.append((copy, when))

        def arrived(which, when):
            when(
                pltpu.make_async_copy(blocks.at[which], blocks.at[which], recv_sems.at[which]).wait
            )

        return started, send, arrived

    g_started, g_move, g_arrived = sender(g_blocks, g_send, g_recv)
    m_started, m_move, m_arrived = sender(m_blocks, m_send, m_recv)

    def send_own(move):
        for k, way in steps:
            move(row, index(a + way * k, b, c), pl.when(inside(a + way * k)))
        for p in b_peers:
            move(row, index(a, p, c), always)
        for p in c_peers:
            move(row, index(a, b, p), always)

    def from_outer(k, way, move, landed):
        when = pl.when(inside(a - way * k))
        s = index(a - way * k, b, c)
        landed(s, when)
        for q in b_peers:
            move(s, index(a, q, c), when)
        for q in c_peers:
            move(s, index(a, b, q), when)

    def from_inner(k, way, move, landed):
        when = pl.when(inside(a - way * k)) if k else always
        for p in b_peers:
            s = index(a - way * k, p, c)
            landed(s, when)
            for q in c_peers:
                move(s, index(a, b, q), when)

    def from_cores(landed):
        for q in c_peers:
            for p in range(outer):
                for r in range(inner):
                    landed(index(p, r, q), always)

    loads[0].wait()
    pl.semaphore_wait(barrier, len(partners))
    send_own(g_move)

    for load in loads[1:5]:
        load.wait()
    levels = lax.broadcasted_iota(jnp.int32, (1, rank), 1)
    for j in range(m_tiles):
        part = jnp.dot(
            top[:, j * order : (j + 1) * order],
            right[j * order : (j + 1) * order, :],
            preferred_element_type=jnp.float32,
        )
        part = jnp.where(levels < col_ranks[j], part, 0.0)
        m_blocks[row, :, j * rank : (j + 1) * rank] = part.astype(jnp.bfloat16)
    send_own(m_move)

    for k, way in steps[:2]:
        from_outer(k, way, g_move, g_arrived)

    for load in loads[5:]:
        load.wait()
    rows = lax.broadcasted_iota(jnp.int32, (rank, 1), 0)
    for i in range(n_tiles):
        part = lax.dot_general(
            bases[i * order : (i + 1) * order, :],
            left[i * order : (i + 1) * order, :],
            (((0,), (0,)), ((), ())),
            preferred_element_type=jnp.float32,
        )
        part = jnp.where(rows < row_ranks[i], part, 0.0)
        cores_k[col, i] = part.astype(jnp.bfloat16)
    k_copies = []
    for number, p in enumerate(col_peers):
        copy = pltpu.make_async_remote_copy(
            src_ref=cores_k.at[col],
            dst_ref=cores_k.at[col],
            send_sem=k_send.at[number],
            recv_sem=k_recv.at[col],
            device_id=(row, p),
            device_id_type=MESH,
        )
        copy.start()
        k_copies.append(copy)

    from_inner(0, 1, g_move, g_arrived)
    for k, way in steps[2:4]:
        from_outer(k, way, g_move, g_arrived)
    for k, way in steps[:2]:
        from_outer(k, way, m_move, m_arrived)
        from_inner(k, way, g_move, g_arrived)
    from_inner(0, 1, m_move, m_arrived)
    for k, way in steps[4:]:
        from_outer(k, way, g_move, g_arrived)
    for number, (k, way) in enumerate(steps[2:]):
        from_outer(k, way, m_move, m_arrived)
        from_inner(k, way, g_move, g_arrived)
        from_inner(*steps[number], m_move, m_arrived)
    for k, way in steps[-2:]:
        from_inner(k, way, m_move, m_arrived)

    from_cores(g_arrived)
    solved = jnp.dot(
        inverse[...],
        g_blocks[...].reshape(order, g_blocks.shape[2]),
        preferred_element_type=jnp.float32,
    ).astype(jnp.bfloat16)
    for p in col_peers:
        pltpu.make_async_copy(cores_k.at[p], cores_k.at[p], k_recv.at[p]).wait()
    for i in range(n_tiles):
        total = jnp.zeros((rank, solved.shape[1]), jnp.float32)
        for k in range(n_col):
            total += jnp.dot(
                cores_k[k, i],
                solved[k * width : (k + 1) * width],
                preferred_element_type=jnp.float32,
            )
        reduced_out[i] = total.astype(jnp.bfloat16)

    stores = [pltpu.make_async_copy(reduced_out, reduced_hbm, store_sem.at[n_tiles])]
    stores[0].start()

    from_cores(m_arrived)
    depth, m_width = m_blocks.shape[1:]
    share = n_row // n_col
    for i in range(n_tiles):
        total = jnp.zeros((rank, m_width), jnp.float32)
        for k in range(n_col):
            piece = m_blocks[k * share : (k + 1) * share]
            total += jnp.dot(
                cores_k[k, i],
                piece.reshape(share * depth, m_width),
                preferred_element_type=jnp.float32,
            )
        core_out[i] = total.astype(jnp.bfloat16)
        store = pltpu.make_async_copy(core_out.at[i], core_hbm.at[i], store_sem.at[i])
        store.start()
        stores.append(store)

    for copy, when in g_started + m_started:
        when(copy.wait_send)
    for copy in k_copies:
        copy.wait_send()
    for store in stores:
        store.wait()


def update_kernel(
    core_hbm,
    reduced_hbm,
    bases_hbm,
    right_hbm,
    slab_hbm,
    rhs_hbm,
    slab_out_hbm,
    rhs_out_hbm,
    core,
    reduced,
    bases,
    right,
    slab,
    rhs,
    slab_out,
    rhs_out,
    load_sem,
    in_sem,
    out_sem,
):
    n_tiles, rank, wide = core.shape
    m_tiles = wide // rank
    order = bases.shape[0] // n_tiles
    chunks = [
        (pl.ds(i * order, order), pl.ds(j * order, order))
        for i in range(n_tiles)
        for j in range(m_tiles)
    ]
    first = [
        pltpu.make_async_copy(core_hbm, core, load_sem.at[3]),
        pltpu.make_async_copy(bases_hbm, bases, load_sem.at[0]),
        pltpu.make_async_copy(right_hbm, right, load_sem.at[1]),
    ]
    later = [
        pltpu.make_async_copy(rhs_hbm, rhs, load_sem.at[2]),
        pltpu.make_async_copy(reduced_hbm, reduced, load_sem.at[4]),
    ]
    loads = [
        pltpu.make_async_copy(slab_hbm.at[at], slab.at[at], in_sem.at[number])
        for number, at in enumerate(chunks)
    ]
    stores = [
        pltpu.make_async_copy(slab_out.at[at], slab_out_hbm.at[at], out_sem.at[number])
        for number, at in enumerate(chunks)
    ]
    for load in first + loads + later:
        load.start()
    for load in first:
        load.wait()
    for number, (at_row, at_col) in enumerate(chunks):
        i, j = number // m_tiles, number % m_tiles
        spread = jnp.dot(
            bases[at_row, :],
            core[i, :, j * rank : (j + 1) * rank],
            preferred_element_type=jnp.float32,
        ).astype(jnp.bfloat16)
        change = lax.dot_general(
            spread,
            right[at_col, :],
            (((1,), (1,)), ((), ())),
            preferred_element_type=jnp.float32,
        )
        loads[number].wait()
        slab_out[at_row, at_col] = (slab[at_row, at_col].astype(jnp.float32) - change).astype(
            jnp.bfloat16
        )
        stores[number].start()
    for load in later:
        load.wait()
    for i in range(n_tiles):
        at = pl.ds(i * order, order)
        lowered = jnp.dot(bases[at, :], reduced[i], preferred_element_type=jnp.float32)
        rhs_out[at, :] = (rhs[at, :].astype(jnp.float32) - lowered).astype(jnp.bfloat16)
        store = pltpu.make_async_copy(
            rhs_out.at[at], rhs_out_hbm.at[at], out_sem.at[len(chunks) + i]
        )
        store.start()
        stores.append(store)
    for store in stores:
        store.wait()


def per_device(
    n_row,
    n_col,
    slab,
    panel_left,
    panel_top,
    row_bases,
    col_bases,
    row_ranks,
    col_ranks,
    pivot_inverse,
    pivot_rhs,
    rhs,
):
    order = pivot_inverse.shape[0]
    rank = row_bases.shape[1]
    n_tiles = row_ranks.shape[0]
    m_tiles = col_ranks.shape[0]
    gains = rhs.shape[1]
    width = panel_left.shape[1]
    outer, inner, cores = grid_of(n_row)
    slots = 2 * outer - 1
    sends = 2 * (outer - 1) + slots * (inner - 1) + slots * inner * (cores - 1)
    hbm = pl.BlockSpec(memory_space=pltpu.HBM)
    core, reduced = pl.pallas_call(
        functools.partial(gather_kernel, n_row, n_col),
        out_shape=(
            jax.ShapeDtypeStruct((n_tiles, rank, m_tiles * rank), jnp.bfloat16),
            jax.ShapeDtypeStruct((n_tiles, rank, gains), jnp.bfloat16),
        ),
        in_specs=[hbm] * 8,
        out_specs=(hbm, hbm),
        scratch_shapes=[
            pltpu.VMEM((n_tiles, rank, m_tiles * rank), jnp.bfloat16),
            pltpu.VMEM((n_tiles, rank, gains), jnp.bfloat16),
            pltpu.SMEM(col_ranks.shape, col_ranks.dtype),
            pltpu.SMEM(row_ranks.shape, row_ranks.dtype),
            pltpu.VMEM(panel_top.shape, jnp.bfloat16),
            pltpu.VMEM(col_bases.shape, jnp.bfloat16),
            pltpu.VMEM(panel_left.shape, jnp.bfloat16),
            pltpu.VMEM(row_bases.shape, jnp.bfloat16),
            pltpu.VMEM(pivot_inverse.shape, jnp.bfloat16),
            pltpu.VMEM((n_row, panel_top.shape[0], m_tiles * rank), jnp.bfloat16),
            pltpu.VMEM((n_row, pivot_rhs.shape[0], gains), jnp.bfloat16),
            pltpu.VMEM((n_col, n_tiles, rank, width), jnp.bfloat16),
            pltpu.SemaphoreType.DMA((8,)),
            pltpu.SemaphoreType.DMA((n_tiles + 1,)),
            pltpu.SemaphoreType.DMA((sends,)),
            pltpu.SemaphoreType.DMA((n_row,)),
            pltpu.SemaphoreType.DMA((sends,)),
            pltpu.SemaphoreType.DMA((n_row,)),
            pltpu.SemaphoreType.DMA((max(n_col - 1, 1),)),
            pltpu.SemaphoreType.DMA((n_col,)),
        ],
        compiler_params=pltpu.CompilerParams(
            collective_id=0, has_side_effects=True, vmem_limit_bytes=62 * 2**20
        ),
        name="gather",
    )(col_ranks, row_ranks, panel_top, col_bases, panel_left, row_bases, pivot_inverse, pivot_rhs)

    return pl.pallas_call(
        update_kernel,
        out_shape=(
            jax.ShapeDtypeStruct(slab.shape, slab.dtype),
            jax.ShapeDtypeStruct(rhs.shape, rhs.dtype),
        ),
        in_specs=[hbm] * 6,
        out_specs=(hbm, hbm),
        scratch_shapes=[
            pltpu.VMEM(core.shape, jnp.bfloat16),
            pltpu.VMEM(reduced.shape, jnp.bfloat16),
            pltpu.VMEM(row_bases.shape, jnp.bfloat16),
            pltpu.VMEM(col_bases.shape, jnp.bfloat16),
            pltpu.VMEM(slab.shape, jnp.bfloat16),
            pltpu.VMEM(rhs.shape, jnp.bfloat16),
            pltpu.VMEM(slab.shape, jnp.bfloat16),
            pltpu.VMEM(rhs.shape, jnp.bfloat16),
            pltpu.SemaphoreType.DMA((5,)),
            pltpu.SemaphoreType.DMA((n_tiles * m_tiles,)),
            pltpu.SemaphoreType.DMA((n_tiles * m_tiles + n_tiles,)),
        ],
        compiler_params=pltpu.CompilerParams(vmem_limit_bytes=62 * 2**20),
        name="update",
    )(core, reduced, row_bases, col_bases, slab, rhs)


def solution(mesh):
    in_specs = (
        P("row", "col"),
        P("row", "col"),
        P("row", "col"),
        P("row", None),
        P("col", None),
        P("row"),
        P("col"),
        P(),
        P("row", "col"),
        P("row", "col"),
    )
    out_specs = (P("row", "col"), P("row", "col"))
    return jax.shard_map(
        functools.partial(per_device, mesh.shape["row"], mesh.shape["col"]),
        mesh=mesh,
        in_specs=in_specs,
        out_specs=out_specs,
        check_vma=False,
    )
```
